128 devices in a mesh: row: 8 (over z, core), col: 16 (over x, y).
Axes of the slice: x: 4, y: 4, z: 4, core: 2. Of those that a mesh axis runs over, the one named last changes fastest.
Arguments:
- layer_input: bfloat16 [1536, 6144], P('col', 'row'), may hold values from -6 to 6
- out_grad: bfloat16 [1536, 6144], P('col', 'row'), may hold values from -6 to 6
- preactivation: bfloat16 [1536, 24576], P('row', 'col'), may hold values from -8 to 8
- weight_in: bfloat16 [6144, 24576], P('row', 'col'), may hold values from -0.078125 to 0.078125
- weight_out: bfloat16 [24576, 6144], P('col', 'row'), may hold values from -0.0390625 to 0.0390625
Outputs:
- input_grad: bfloat16 [1536, 6144], P('col', 'row')
- weight_in_grad: float32 [6144, 24576], P('row', 'col')
- weight_out_grad: float32 [24576, 6144], P('col', 'row')
The draws below stay inside these ranges and needn't reach their ends.
All inputs are finite; a program needn't handle non-finite values.
Results may differ from the reference program's by a relative error of at most 0.0049.
Values may be sent and summed in bfloat16 or wider, within the bound.
No kernel may reach another device: no remote copies, remote signals or barrier semaphores. Data moves between devices by JAX's collectives and lax.ppermute only.
A program may use at most 128 MiB of HBM per device.

```python
import jax
import jax.numpy as jnp
from jax import lax

D = 6144
F = 24576
TOKENS = 1536


def level_of(stream_key, shape, split, low, top_value):
    loudness = 1.0
    for axis_at, shards_of in split:
        draws = jax.random.uniform(jax.random.fold_in(jax.random.fold_in(stream_key, 6), axis_at), (shards_of,), jnp.float32, low / len(split), top_value / len(split))
        loudness = loudness * jnp.repeat(jnp.exp(draws), shape[axis_at] // shards_of).reshape((-1,) + (1,) * (len(shape) - 1 - axis_at))
    return loudness


def bell_draw(rng, dims, width, most, shards=(), held_as=jnp.bfloat16):
    values = jax.random.normal(rng, dims, jnp.float32) * width
    if len(shards) > 0:
        values = level_of(rng, dims, shards, -0.22, 0.18) * values
    return jnp.clip(values, min=-most, max=most).astype(held_as)


def setup_inputs(seed: int = 0) -> dict:
    key_of = jax.random.split(jax.random.key(seed), 6)
    return {
        "layer_input": bell_draw(key_of[0], (TOKENS, D), 1.0, 6.0, ((0, 16), (1, 8))),
        "out_grad": bell_draw(key_of[1], (TOKENS, D), 1.0, 6.0, ((0, 16), (1, 8))),
        "preactivation": bell_draw(key_of[2], (TOKENS, F), 1.5, 8.0, ((0, 8), (1, 16))),
        "weight_in": bell_draw(key_of[3], (D, F), D ** -0.5, 0.078125, ((0, 8), (1, 16))),
        "weight_out": bell_draw(key_of[4], (F, D), F ** -0.5, 0.0390625, ((0, 16), (1, 8))),
    }


coeff = 0.7978845608
cubic = 0.044715


def gelu_parts(before):
    inner = coeff * (before + cubic * before * before * before)
    tanh_value = jnp.tanh(inner)
    value = 0.5 * before * (1.0 + tanh_value)
    slope = 0.5 * (1.0 + tanh_value) + 0.5 * before * (1.0 - tanh_value * tanh_value) * coeff * (1.0 + 3.0 * cubic * before * before)
    return value, slope


def reference(layer_input, out_grad, preactivation, weight_in, weight_out):
    before = preactivation.astype(jnp.float32)
    value, slope = gelu_parts(before)
    activation = value.astype(jnp.bfloat16)
    act_grad = lax.dot_general(out_grad, weight_out, (((1,), (1,)), ((), ())), preferred_element_type=jnp.float32)
    hidden_grad = (act_grad * slope).astype(jnp.bfloat16)
    input_grad = lax.dot_general(hidden_grad, weight_in, (((1,), (1,)), ((), ())), preferred_element_type=jnp.float32).astype(jnp.bfloat16)
    weight_in_grad = lax.dot_general(layer_input, hidden_grad, (((0,), (0,)), ((), ())), preferred_element_type=jnp.float32)
    weight_out_grad = lax.dot_general(activation, out_grad, (((0,), (0,)), ((), ())), preferred_element_type=jnp.float32)
    return input_grad, weight_in_grad, weight_out_grad
```

```python
import jax
import jax.numpy as jnp
from jax import lax
from jax.experimental import pallas as pl
from jax.experimental.pallas import tpu as pltpu
from jax.sharding import PartitionSpec as P

coeff = 0.7978845608
cubic = 0.044715

N = 4
K = 48
VMEM = 56 * 2**20
LIGHT = pl.CostEstimate(flops=1024, bytes_accessed=1024, transcendentals=0)
AXES = ("row", "col")
BF = jnp.bfloat16
F32 = jnp.float32


def permute(array, target):
    pairs = []
    for z in range(N):
        for c in range(2):
            for x in range(N):
                for y in range(N):
                    tz, tc, tx, ty = target(z, c, x, y)
                    to = (((tz % N) * 2 + tc) * N + tx % N) * N + ty % N
                    pairs.append((((z * 2 + c) * N + x) * N + y, to))
    return lax.ppermute(array, AXES, pairs)


def swap(array):
    return permute(array, lambda z, c, x, y: (z, 1 - c, x, y))


def along_z(array, by):
    return permute(array, lambda z, c, x, y: (z + by, c, x, y))


def first_ring(array, by):
    return permute(array, lambda z, c, x, y: (z, c, x, y + by) if c else (z, c, x + by, y))


def second_ring(array, by):
    return permute(array, lambda z, c, x, y: (z, c, x + by, y) if c else (z, c, x, y + by))


def gelu_parts(before):
    inner = coeff * (before + cubic * before * before * before)
    tanh_value = jnp.tanh(inner)
    value = 0.5 * before * (1.0 + tanh_value)
    slope = 0.5 * (1.0 + tanh_value) + 0.5 * before * (1.0 - tanh_value * tanh_value) * coeff * (
        1.0 + 3.0 * cubic * before * before
    )
    return (value, slope)


def gather_z(block):
    below = along_z(block, 1)
    above = along_z(block, -1)
    far_a = along_z(below[:2], 1)
    far_b = along_z(above[2:], -1)
    return [block, above, far_a, far_b, below]


def place_xy(where, core, q, r):
    dx = jnp.where(core == 0, r, q)
    dy = jnp.where(core == 0, q, r)
    return ((where[2] + dx) % N, (where[3] + dy) % N)


def dot_nt(a, b):
    return lax.dot_general(a, b, (((1,), (1,)), ((), ())), preferred_element_type=F32)


def dot_tn(a, b):
    return lax.dot_general(a, b, (((0,), (0,)), ((), ())), preferred_element_type=F32)


ANY = pl.BlockSpec(memory_space=pl.ANY)
STEPS = 3


def act_grad_kernel(where, *refs):
    own, other, weights = refs[0:4], refs[4:8], refs[8:10]
    outs = refs[10:14]
    lhs, w, p0, p1, in_sems, w_sems, out_sems = refs[14:]
    rows = w.shape[1] // STEPS
    loads = []
    for j in range(STEPS):
        part = pl.ds(j * rows, rows)
        for half in range(2):
            loads.append(pltpu.make_async_copy(weights[half].at[part], w.at[half, part], w_sems.at[j, half]))
    fills = []
    mine = pl.ds(pl.multiple_of(where[1] * K, 16), K)
    for half, stacks in enumerate((own, other)):
        for q, stack in enumerate(stacks):
            for r in range(N):
                x, y = place_xy(where, where[1] if half == 0 else 1 - where[1], q, r)
                to = lhs.at[half, (x + N - where[0]) % N, y]
                fills.append(pltpu.make_async_copy(stack.at[r, mine], to, in_sems.at[half, q, r]))
    for copy in loads[:2] + fills + loads[2:]:
        copy.start()
    for copy in fills:
        copy.wait()
    stores = []
    for j in range(STEPS):
        loads[2 * j].wait()
        loads[2 * j + 1].wait()
        part = pl.ds(j * rows, rows)
        total = dot_nt(lhs[0].reshape(16 * K, -1), w[0, part]) + dot_nt(lhs[1].reshape(16 * K, -1), w[1, part])
        p0[:, part] = total[: N * K]
        for r in (1, 2, 3):
            p1[r - 1, :, part] = total[r * N * K : (r + 1) * N * K].astype(BF)
        for r in range(N):
            source = p0.at[:, part] if r == 0 else p1.at[r - 1, :, part]
            stores.append(pltpu.make_async_copy(source, outs[r].at[:, part], out_sems.at[j, r]))
            stores[-1].start()
    for copy in stores:
        copy.wait()


def act_grad_parts(where, stacks, others, w_own, w_other):
    hidden, half = w_own.shape
    return pl.pallas_call(
        act_grad_kernel,
        out_shape=[jax.ShapeDtypeStruct((N * K, hidden), t) for t in (F32, BF, BF, BF)],
        grid_spec=pltpu.PrefetchScalarGridSpec(
            num_scalar_prefetch=1,
            grid=(),
            in_specs=[ANY] * 10,
            out_specs=[ANY] * 4,
            scratch_shapes=[
                pltpu.VMEM((2, N, N, K, half), BF),
                pltpu.VMEM((2, hidden, half), BF),
                pltpu.VMEM((N * K, hidden), F32),
                pltpu.VMEM((3, N * K, hidden), BF),
                pltpu.SemaphoreType.DMA((2, N, N)),
                pltpu.SemaphoreType.DMA((STEPS, 2)),
                pltpu.SemaphoreType.DMA((STEPS, N)),
            ],
        ),
        compiler_params=pltpu.CompilerParams(vmem_limit_bytes=VMEM),
        cost_estimate=LIGHT,
        name="act_grad",
    )(where, *stacks, *others, w_own, w_other)


def input_grad_kernel(where, h0, h1, h2a, h2b, h3, w_own, w_other, *refs):
    outs, (rows_out, lhs, w, near, far, in_sems, w_sems, out_sems) = refs[:4], refs[4:]
    n = h0.shape[1]
    half = w_own.shape[0]
    rows = half // STEPS
    loads = []
    for j in range(2 * STEPS):
        weight = (w_own, w_other)[j // STEPS]
        loads.append(
            pltpu.make_async_copy(
                weight.at[pl.ds(j % STEPS * rows, rows)], w.at[pl.ds(j * rows, rows)], w_sems.at[j]
            )
        )
    fills = []
    for zr in range(N):
        for y in range(N):
            if zr == 2:
                piece = (h2a, h2b)[y // 2].at[y % 2]
            else:
                piece = (h0, h1, None, h3)[zr].at[y]
            dx = (where[0] + zr + N - where[2]) % N
            dy = (y + N - where[3]) % N
            r = jnp.where(where[1] == 0, dx, dy)
            q = jnp.where(where[1] == 0, dy, dx)
            fills.append(pltpu.make_async_copy(piece, lhs.at[r, q], in_sems.at[zr, y]))
    for copy in loads[:1] + fills + loads[1:]:
        copy.start()
    for copy in fills:
        copy.wait()
    stores = [pltpu.make_async_copy(lhs, rows_out, out_sems.at[2 * STEPS, 0])]
    stores[0].start()
    for j in range(2 * STEPS):
        loads[j].wait()
        part = pl.ds(j * rows, rows)
        total = dot_nt(lhs[...].reshape(16 * n, -1), w[part]).reshape(N, N, n, -1)
        near[:, :, part] = total[0]
        for r in (1, 2, 3):
            far[r - 1, :, :, part] = total[r].astype(BF)
        for r in range(N):
            source = near.at[:, :, part] if r == 0 else far.at[r - 1, :, :, part]
            stores.append(pltpu.make_async_copy(source, outs[r].at[:, :, part], out_sems.at[j, r]))
            stores[-1].start()
    for copy in stores:
        copy.wait()


def input_grad_parts(where, pieces, w_own, w_other):
    half, hidden = w_own.shape
    n = pieces[0].shape[1]
    return pl.pallas_call(
        input_grad_kernel,
        out_shape=[jax.ShapeDtypeStruct((N, n, 2 * half), t) for t in (F32, BF, BF, BF)]
        + [jax.ShapeDtypeStruct((N, N, n, hidden), BF)],
        grid_spec=pltpu.PrefetchScalarGridSpec(
            num_scalar_prefetch=1,
            grid=(),
            in_specs=[ANY] * 7,
            out_specs=[ANY] * 5,
            scratch_shapes=[
                pltpu.VMEM((N, N, n, hidden), BF),
                pltpu.VMEM((2 * half, hidden), BF),
                pltpu.VMEM((N, n, 2 * half), F32),
                pltpu.VMEM((3, N, n, 2 * half), BF),
                pltpu.SemaphoreType.DMA((N, N)),
                pltpu.SemaphoreType.DMA((2 * STEPS,)),
                pltpu.SemaphoreType.DMA((2 * STEPS + 1, N)),
            ],
        ),
        compiler_params=pltpu.CompilerParams(vmem_limit_bytes=VMEM),
        cost_estimate=LIGHT,
        name="input_grad",
    )(where, *pieces, w_own, w_other)


def weight_out_grad_kernel(where, act, g0, g1, g2, g3, out, rhs, sems):
    @pl.when(pl.program_id(0) == 0)
    def _():
        work = []
        for q, stack in enumerate((g0, g1, g2, g3)):
            for r in range(N):
                x, y = place_xy(where, where[1], q, r)
                work.append(pltpu.make_async_copy(stack.at[r], rhs.at[x, y], sems.at[q, r]))
        for copy in work:
            copy.start()
        for copy in work:
            copy.wait()

    out[...] = dot_tn(act[...], rhs[...].reshape(32 * K, -1))


def weight_out_grad_of(where, act, stacks):
    tokens, hidden = act.shape
    width = stacks[0].shape[-1]
    block = 512
    return pl.pallas_call(
        weight_out_grad_kernel,
        out_shape=jax.ShapeDtypeStruct((hidden, width), F32),
        grid_spec=pltpu.PrefetchScalarGridSpec(
            num_scalar_prefetch=1,
            grid=(hidden // block,),
            in_specs=[pl.BlockSpec((tokens, block), lambda i, s: (0, i))] + [ANY] * 4,
            out_specs=pl.BlockSpec((block, width), lambda i, s: (i, 0)),
            scratch_shapes=[pltpu.VMEM((N, N, 2 * K, width), BF), pltpu.SemaphoreType.DMA((N, N))],
        ),
        compiler_params=pltpu.CompilerParams(vmem_limit_bytes=VMEM),
        cost_estimate=LIGHT,
        name="weight_out_grad",
    )(where, act, *stacks)


def weight_in_grad_kernel(where, inputs, hid_own, hid_other, out, lhs):
    @pl.when(pl.program_id(0) == 0)
    def _():
        for s in range(2):
            core = where[1] if s == 0 else 1 - where[1]
            for r in range(N):
                for q in range(N):
                    x, y = place_xy(where, core, q, r)
                    lhs[s, r, q] = inputs[x * N + y, core]

    rows = lhs[...].reshape(2, 16 * K, -1)
    out[...] = dot_tn(rows[0], hid_own[...]) + dot_tn(rows[1], hid_other[...])


def weight_in_grad_of(where, inputs, hid_own, hid_other):
    hidden = hid_own.shape[-1]
    width = inputs.shape[1]
    block = 512
    b = pl.BlockSpec((16 * K, block), lambda i, s: (0, i))
    return pl.pallas_call(
        weight_in_grad_kernel,
        out_shape=jax.ShapeDtypeStruct((width, hidden), F32),
        grid_spec=pltpu.PrefetchScalarGridSpec(
            num_scalar_prefetch=1,
            grid=(hidden // block,),
            in_specs=[pl.BlockSpec((16, 2, K, width), lambda i, s: (0, 0, 0, 0)), b, b],
            out_specs=pl.BlockSpec((width, block), lambda i, s: (0, i)),
            scratch_shapes=[pltpu.VMEM((2, N, N, K, width), BF)],
        ),
        compiler_params=pltpu.CompilerParams(vmem_limit_bytes=VMEM),
        cost_estimate=LIGHT,
        name="weight_in_grad",
    )(where, inputs.reshape(16, 2, K, width), hid_own.reshape(-1, hidden), hid_other.reshape(-1, hidden))


def on_device(layer_input, out_grad, preactivation, weight_in, weight_out):
    row, col = lax.axis_index("row"), lax.axis_index("col")
    core = row % 2
    where = jnp.stack([row // 2, core, col // N, col % N]).astype(jnp.int32)
    width = layer_input.shape[1]
    hidden = preactivation.shape[1]

    def mine_and_other(array, axis):
        mine = lax.dynamic_index_in_dim(array, core, axis, keepdims=False)
        other = lax.dynamic_index_in_dim(array, 1 - core, axis, keepdims=False)
        return mine, swap(other)

    def in_core_order(mine, received, axis):
        return jnp.where(
            core == 0,
            jnp.concatenate([mine, received], axis),
            jnp.concatenate([received, mine], axis),
        )

    hold = lax.optimization_barrier
    w_out_other, w_in_other = swap(weight_out), swap(weight_in)
    g_near = [first_ring(out_grad, -r) for r in (1, 3, 2)]
    w_out_other, preact = hold((w_out_other, preactivation))
    act = gelu_parts(preact.astype(F32))[0].astype(BF)
    act_all = lax.all_gather(act, "row", axis=0, tiled=True)

    g_near, w_out_other, w_in_other, preact = hold((g_near, w_out_other, w_in_other, preact))
    g_stack = jnp.stack([out_grad, g_near[0], g_near[2], g_near[1]])
    g_far = [second_ring(g_stack, -q) for q in (1, 3, 2)]
    h_set = in_core_order(*mine_and_other(preact.reshape(2, 2, K, hidden), 1), 0)
    slope = gelu_parts(h_set.astype(F32))[1]
    g_far, slope = hold((g_far, slope))
    g_stacks = [g_stack, g_far[0], g_far[2], g_far[1]]
    g_others = [swap(g) for g in g_stacks]

    p0, p1, p2, p3 = act_grad_parts(where, g_stacks, g_others, weight_out, w_out_other)
    x_late, g_stacks = hold((layer_input, g_stacks))
    x_all = lax.all_gather(x_late, "col", axis=0, tiled=True)
    weight_out_grad = weight_out_grad_of(where, act_all, g_stacks)
    s1, s3, s2, weight_out_grad = hold((along_z(p1, 1), along_z(p3, -1), along_z(p2, 2), weight_out_grad))

    act_grad = (p0 + s1.astype(F32) + s2.astype(F32) + s3.astype(F32)).reshape(N, K, hidden)
    pieces = gather_z((act_grad * slope).astype(BF))
    d0, d1, d2, d3, hid_own = input_grad_parts(where, pieces, weight_in, w_in_other)
    got = [first_ring(d, r) for r, d in ((1, d1), (3, d3), (2, d2))]
    weight_in_grad = weight_in_grad_of(where, x_all, hid_own, swap(hid_own))
    got, weight_in_grad = hold((got, weight_in_grad))

    e = d0 + got[0].astype(F32) + got[1].astype(F32) + got[2].astype(F32)
    total = e[0]
    for q in (1, 3, 2):
        total = total + second_ring(e[q].astype(BF), q).astype(F32)
    total = total.astype(BF)
    input_grad = in_core_order(total[:, :width], swap(total[:, width:]), 0)
    return (input_grad, weight_in_grad, weight_out_grad)


def solution(mesh):
    placed = (P("col", "row"), P("col", "row"), P("row", "col"), P("row", "col"), P("col", "row"))
    return jax.shard_map(
        on_device,
        mesh=mesh,
        in_specs=placed,
        out_specs=(P("col", "row"), P("row", "col"), P("col", "row")),
        check_vma=False,
    )
```

```python
import functools

import jax
import jax.numpy as jnp
from jax import lax
from jax.experimental import pallas as pl
from jax.experimental.pallas import tpu as pltpu
from jax.sharding import PartitionSpec as P

coeff = 0.7978845608
cubic = 0.044715

N = 4
K = 48
VMEM = 56 * 2**20
SMALL = 48 * 2**20
LIGHT = pl.CostEstimate(flops=1024, bytes_accessed=1024, transcendentals=0)
HEAVY = pl.CostEstimate(flops=8 * 10**9, bytes_accessed=2**24, transcendentals=0)
AXES = ("row", "col")
BF = jnp.bfloat16
F32 = jnp.float32


def permute(array, target):
    pairs = []
    for z in range(N):
        for c in range(2):
            for x in range(N):
                for y in range(N):
                    tz, tc, tx, ty = target(z, c, x, y)
                    to = (((tz % N) * 2 + tc) * N + tx % N) * N + ty % N
                    pairs.append((((z * 2 + c) * N + x) * N + y, to))
    return lax.ppermute(array, AXES, pairs)


def swap(array):
    return permute(array, lambda z, c, x, y: (z, 1 - c, x, y))


def along_z(array, by):
    return permute(array, lambda z, c, x, y: (z + by, c, x, y))


def first_ring(array, by):
    return permute(array, lambda z, c, x, y: (z, c, x, y + by) if c else (z, c, x + by, y))


def second_ring(array, by):
    return permute(array, lambda z, c, x, y: (z, c, x + by, y) if c else (z, c, x, y + by))


def gelu_parts(before):
    inner = coeff * (before + cubic * before * before * before)
    tanh_value = jnp.tanh(inner)
    value = 0.5 * before * (1.0 + tanh_value)
    slope = 0.5 * (1.0 + tanh_value) + 0.5 * before * (1.0 - tanh_value * tanh_value) * coeff * (
        1.0 + 3.0 * cubic * before * before
    )
    return (value, slope)


def place_xy(where, core, q, r):
    dx = jnp.where(core == 0, r, q)
    dy = jnp.where(core == 0, q, r)
    return ((where[2] + dx) % N, (where[3] + dy) % N)


def dot_nt(a, b):
    return lax.dot_general(a, b, (((1,), (1,)), ((), ())), preferred_element_type=F32)


def dot_tn(a, b):
    return lax.dot_general(a, b, (((0,), (0,)), ((), ())), preferred_element_type=F32)


HBM = pl.BlockSpec(memory_space=pltpu.HBM)
ANY = pl.BlockSpec(memory_space=pl.ANY)


def relay_slot(zr, y):
    low = y < 2
    up = jnp.where(low, 12 + y, y)
    far = jnp.where(low, y, 4 + y)
    down = jnp.where(low, 4 + y, 12 + y)
    return jnp.where(zr == 0, 8 + y, jnp.where(zr == 1, up, jnp.where(zr == 2, far, down)))


def act_grad_kernel(part, where, *refs):
    own, other, weights, outs = refs[0:4], refs[4:8], refs[8:10], refs[10:12]
    lhs, w, staged, in_sems, w_sems, out_sems = refs[12:]
    columns = w.shape[2]
    loads = [
        pltpu.make_async_copy(weights[half].at[pl.ds(f * columns, columns)], w.at[f, half], w_sems.at[f, half])
        for f in range(2)
        for half in range(2)
    ]
    fills = []
    mine = pl.ds(pl.multiple_of(where[1] * K, 16), K)
    for half, stacks in enumerate((own, other)):
        for q, stack in enumerate(stacks):
            for r in range(N):
                x, y = place_xy(where, where[1] if half == 0 else 1 - where[1], q, r)
                slot = relay_slot((x + N - where[0]) % N, y) - 8 * part
                to = lhs.at[half, jnp.clip(slot, 0, 7)]
                copy = pltpu.make_async_copy(stack.at[r, mine], to, in_sems.at[half, q, r])
                fills.append(((slot >= 0) & (slot < 8), copy))
    for copy in loads[:2]:
        copy.start()
    for wanted, copy in fills:
        pl.when(wanted)(copy.start)
    for copy in loads[2:]:
        copy.start()
    for wanted, copy in fills:
        pl.when(wanted)(copy.wait)
    a, b = (lhs[half].reshape(8 * K, -1) for half in range(2))
    stores = []
    for f in range(2):
        loads[2 * f].wait()
        loads[2 * f + 1].wait()
        total = dot_nt(a, w[f, 0]) + dot_nt(b, w[f, 1])
        at = pl.ds(f * columns, columns)
        staged[:, :, at] = total.reshape(2, N * K, columns).astype(staged.dtype)
        for i in range(2):
            stores.append(pltpu.make_async_copy(staged.at[i, :, at], outs[i].at[:, at], out_sems.at[f, i]))
            stores[-1].start()
    for copy in stores:
        copy.wait()


def act_grad_parts(part, where, stacks, others, w_own, w_other):
    hidden, half = w_own.shape
    kind = (BF, F32)[part]
    return pl.pallas_call(
        functools.partial(act_grad_kernel, part),
        out_shape=[jax.ShapeDtypeStruct((N * K, hidden), kind)] * 2,
        grid_spec=pltpu.PrefetchScalarGridSpec(
            num_scalar_prefetch=1,
            grid=(),
            in_specs=[ANY] * 8 + [HBM, ANY],
            out_specs=[ANY] * 2,
            scratch_shapes=[
                pltpu.VMEM((2, 8, K, half), BF),
                pltpu.VMEM((2, 2, hidden // 2, half), BF),
                pltpu.VMEM((2, N * K, hidden), kind),
                pltpu.SemaphoreType.DMA((2, N, N)),
                pltpu.SemaphoreType.DMA((2, 2)),
                pltpu.SemaphoreType.DMA((2, 2)),
            ],
        ),
        compiler_params=pltpu.CompilerParams(vmem_limit_bytes=SMALL),
        cost_estimate=HEAVY if part else LIGHT,
        name="act_grad",
    )(where, *stacks, *others, w_own, w_other)


def input_grad_kernel(where, h0, h1, h2a, h2b, h3, w_own, w_other, *refs):
    outs, (rows_out, lhs, w, near, far, in_sems, w_sems, out_sems) = refs[:4], refs[4:]
    n = h0.shape[1]
    half = w_own.shape[0]
    rows = half
    loads = []
    for j in range(2):
        weight = (w_own, w_other)[j]
        loads.append(pltpu.make_async_copy(weight, w.at[pl.ds(j * rows, rows)], w_sems.at[j]))
    fills = []
    for zr in range(N):
        for y in range(N):
            if zr == 2:
                piece = (h2a, h2b)[y // 2].at[y % 2]
            else:
                piece = (h0, h1, None, h3)[zr].at[y]
            dx = (where[0] + zr + N - where[2]) % N
            dy = (y + N - where[3]) % N
            r = jnp.where(where[1] == 0, dx, dy)
            q = jnp.where(where[1] == 0, dy, dx)
            fills.append(pltpu.make_async_copy(piece, lhs.at[r, q], in_sems.at[zr, y]))
    for copy in loads[:1] + fills + loads[1:]:
        copy.start()
    for copy in fills:
        copy.wait()
    stores = [pltpu.make_async_copy(lhs, rows_out, out_sems.at[2, 0])]
    stores[0].start()
    for j in range(2):
        loads[j].wait()
        part = pl.ds(j * rows, rows)
        total = dot_nt(lhs[...].reshape(16 * n, -1), w[part]).reshape(N, N, n, -1)
        near[:, :, part] = total[0]
        for r in (1, 2, 3):
            far[r - 1, :, :, part] = total[r].astype(BF)
        for r in range(N):
            source = near.at[:, :, part] if r == 0 else far.at[r - 1, :, :, part]
            stores.append(pltpu.make_async_copy(source, outs[r].at[:, :, part], out_sems.at[j, r]))
            stores[-1].start()
    for copy in stores:
        copy.wait()


def input_grad_parts(where, pieces, w_own, w_other):
    half, hidden = w_own.shape
    n = pieces[0].shape[1]
    return pl.pallas_call(
        input_grad_kernel,
        out_shape=[jax.ShapeDtypeStruct((N, n, 2 * half), t) for t in (F32, BF, BF, BF)]
        + [jax.ShapeDtypeStruct((N, N, n, hidden), BF)],
        grid_spec=pltpu.PrefetchScalarGridSpec(
            num_scalar_prefetch=1,
            grid=(),
            in_specs=[HBM] * 7,
            out_specs=[HBM] * 5,
            scratch_shapes=[
                pltpu.VMEM((N, N, n, hidden), BF),
                pltpu.VMEM((2 * half, hidden), BF),
                pltpu.VMEM((N, n, 2 * half), F32),
                pltpu.VMEM((3, N, n, 2 * half), BF),
                pltpu.SemaphoreType.DMA((N, N)),
                pltpu.SemaphoreType.DMA((2,)),
                pltpu.SemaphoreType.DMA((3, N)),
            ],
        ),
        compiler_params=pltpu.CompilerParams(vmem_limit_bytes=SMALL),
        cost_estimate=LIGHT,
        name="input_grad",
    )(where, *pieces, w_own, w_other)


def weight_out_grad_kernel(where, act, g0, g1, g2, g3, out, rhs, sems):
    @pl.when(pl.program_id(0) == 0)
    def _():
        work = []
        for q, stack in enumerate((g0, g1, g2, g3)):
            for r in range(N):
                x, y = place_xy(where, where[1], q, r)
                work.append(pltpu.make_async_copy(stack.at[r], rhs.at[x, y], sems.at[q, r]))
        for copy in work:
            copy.start()
        for copy in work:
            copy.wait()

    out[...] = dot_tn(act[...], rhs[...].reshape(32 * K, -1))


def weight_out_grad_of(where, act, stacks):
    tokens, hidden = act.shape
    width = stacks[0].shape[-1]
    block = 512
    return pl.pallas_call(
        weight_out_grad_kernel,
        out_shape=jax.ShapeDtypeStruct((hidden, width), F32),
        grid_spec=pltpu.PrefetchScalarGridSpec(
            num_scalar_prefetch=1,
            grid=(hidden // block,),
            in_specs=[pl.BlockSpec((tokens, block), lambda i, s: (0, i))] + [HBM] * 4,
            out_specs=pl.BlockSpec((block, width), lambda i, s: (i, 0)),
            scratch_shapes=[pltpu.VMEM((N, N, 2 * K, width), BF), pltpu.SemaphoreType.DMA((N, N))],
        ),
        compiler_params=pltpu.CompilerParams(vmem_limit_bytes=VMEM),
        cost_estimate=HEAVY,
        name="weight_out_grad",
    )(where, act, *stacks)


def weight_in_grad_kernel(where, inputs, hid_own, hid_other, out, lhs):
    @pl.when(pl.program_id(0) == 0)
    def _():
        for s in range(2):
            core = where[1] if s == 0 else 1 - where[1]
            for r in range(N):
                for q in range(N):
                    x, y = place_xy(where, core, q, r)
                    lhs[s, r, q] = inputs[x * N + y, core]

    rows = lhs[...].reshape(2, 16 * K, -1)
    out[...] = dot_tn(rows[0], hid_own[...]) + dot_tn(rows[1], hid_other[...])


def weight_in_grad_of(where, inputs, hid_own, hid_other):
    hidden = hid_own.shape[-1]
    width = inputs.shape[1]
    block = 512
    b = pl.BlockSpec((16 * K, block), lambda i, s: (0, i))
    return pl.pallas_call(
        weight_in_grad_kernel,
        out_shape=jax.ShapeDtypeStruct((width, hidden), F32),
        grid_spec=pltpu.PrefetchScalarGridSpec(
            num_scalar_prefetch=1,
            grid=(hidden // block,),
            in_specs=[pl.BlockSpec((16, 2, K, width), lambda i, s: (0, 0, 0, 0)), b, b],
            out_specs=pl.BlockSpec((width, block), lambda i, s: (0, i)),
            scratch_shapes=[pltpu.VMEM((2, N, N, K, width), BF)],
        ),
        compiler_params=pltpu.CompilerParams(vmem_limit_bytes=VMEM),
        cost_estimate=HEAVY,
        name="weight_in_grad",
    )(where, inputs.reshape(16, 2, K, width), hid_own.reshape(-1, hidden), hid_other.reshape(-1, hidden))


def on_device(layer_input, out_grad, preactivation, weight_in, weight_out):
    row, col = lax.axis_index("row"), lax.axis_index("col")
    core = row % 2
    where = jnp.stack([row // 2, core, col // N, col % N]).astype(jnp.int32)
    width = layer_input.shape[1]
    hidden = preactivation.shape[1]

    def mine_and_other(array, axis):
        mine = lax.dynamic_index_in_dim(array, core, axis, keepdims=False)
        other = lax.dynamic_index_in_dim(array, 1 - core, axis, keepdims=False)
        return mine, swap(other)

    def in_core_order(mine, received, axis):
        return jnp.where(
            core == 0,
            jnp.concatenate([mine, received], axis),
            jnp.concatenate([received, mine], axis),
        )

    hold = lax.optimization_barrier
    act = gelu_parts(preactivation.astype(F32))[0].astype(BF)
    act_all = lax.all_gather(act, "row", axis=0, tiled=True)
    g_near = [first_ring(out_grad, -r) for r in (1, 3, 2)]
    w_out_other, w_in_other = swap(weight_out), swap(weight_in)
    g_near, w_out_other, w_in_other, preact, where = hold(
        (g_near, w_out_other, w_in_other, preactivation, where)
    )
    g_stack = jnp.stack([out_grad, g_near[0], g_near[2], g_near[1]])
    g_far = [second_ring(g_stack, -q) for q in (1, 3, 2)]
    h_set = in_core_order(*mine_and_other(preact.reshape(2, 2, K, hidden), 1), 0)
    slope = gelu_parts(h_set.astype(F32))[1]
    g_far[0], slope = hold((g_far[0], slope))
    g_stacks = [g_stack, g_far[0], g_far[2], g_far[1]]
    g_others = [swap(g) for g in g_stacks]

    half = N * K // 2
    to_up, to_down = act_grad_parts(0, where, g_stacks, g_others, weight_out, w_out_other)
    from_down, from_up = along_z(to_up, 1), along_z(to_down, -1)
    g_stacks, g_others, act_all, to_up, x_late = hold((g_stacks, g_others, act_all, to_up, layer_input))
    x_all = lax.all_gather(x_late, "col", axis=0, tiled=True)
    own, relay = act_grad_parts(1, where, g_stacks, g_others, weight_out, w_out_other)
    from_down, from_up, own, relay = hold((from_down, from_up, own, relay))
    relay_up = (relay[:half] + from_down[:half].astype(F32)).astype(BF)
    relay_down = (relay[half:] + from_up[half:].astype(F32)).astype(BF)
    sum_a, sum_b = along_z(relay_up, 1), along_z(relay_down, -1)
    rest = jnp.concatenate([from_up[:half], from_down[half:]]).astype(F32)
    act_grad = own + rest + jnp.concatenate([sum_a, sum_b]).astype(F32)
    hid = (act_grad.reshape(N, K, hidden) * slope).astype(BF)

    below, above = along_z(hid, 1), along_z(hid, -1)
    act_late, hid = hold((act_all, hid))
    weight_out_grad = weight_out_grad_of(where, act_late, g_stacks)
    below, above, weight_out_grad = hold((below, above, weight_out_grad))
    pieces = [hid, above, along_z(below[:2], 1), along_z(above[2:], -1), below]
    d0, d1, d2, d3, hid_own = input_grad_parts(where, pieces, weight_in, w_in_other)
    got = [first_ring(d, r) for r, d in ((1, d1), (3, d3), (2, d2))]
    weight_in_grad = weight_in_grad_of(where, x_all, hid_own, swap(hid_own))
    got, weight_in_grad = hold((got, weight_in_grad))

    e = d0 + got[0].astype(F32) + got[1].astype(F32) + got[2].astype(F32)
    total = e[0]
    for q in (1, 3, 2):
        total = total + second_ring(e[q].astype(BF), q).astype(F32)
    total = total.astype(BF)
    input_grad = in_core_order(total[:, :width], swap(total[:, width:]), 0)
    return (input_grad, weight_in_grad, weight_out_grad)


def solution(mesh):
    placed = (P("col", "row"), P("col", "row"), P("row", "col"), P("row", "col"), P("col", "row"))
    return jax.shard_map(
        on_device,
        mesh=mesh,
        in_specs=placed,
        out_specs=(P("col", "row"), P("row", "col"), P("col", "row")),
        check_vma=False,
    )
```

```python
import functools

import jax
import jax.numpy as jnp
from jax import lax
from jax.experimental import pallas as pl
from jax.experimental.pallas import tpu as pltpu
from jax.sharding import PartitionSpec as P

coeff = 0.7978845608
cubic = 0.044715

N = 4
K = 48
VMEM = 56 * 2**20
SMALL = 48 * 2**20
LIGHT = pl.CostEstimate(flops=1024, bytes_accessed=1024, transcendentals=0)
HEAVY = pl.CostEstimate(flops=8 * 10**9, bytes_accessed=2**24, transcendentals=0)
AXES = ("row", "col")
BF = jnp.bfloat16
F32 = jnp.float32


def permute(array, target):
    pairs = []
    for z in range(N):
        for c in range(2):
            for x in range(N):
                for y in range(N):
                    tz, tc, tx, ty = target(z, c, x, y)
                    to = (((tz % N) * 2 + tc) * N + tx % N) * N + ty % N
                    pairs.append((((z * 2 + c) * N + x) * N + y, to))
    return lax.ppermute(array, AXES, pairs)


def swap(array):
    return permute(array, lambda z, c, x, y: (z, 1 - c, x, y))


def along_z(array, by):
    return permute(array, lambda z, c, x, y: (z + by, c, x, y))


def first_ring(array, by):
    return permute(array, lambda z, c, x, y: (z, c, x, y + by) if c else (z, c, x + by, y))


def second_ring(array, by):
    return permute(array, lambda z, c, x, y: (z, c, x + by, y) if c else (z, c, x, y + by))


def gelu_parts(before):
    inner = coeff * (before + cubic * before * before * before)
    tanh_value = jnp.tanh(inner)
    value = 0.5 * before * (1.0 + tanh_value)
    slope = 0.5 * (1.0 + tanh_value) + 0.5 * before * (1.0 - tanh_value * tanh_value) * coeff * (
        1.0 + 3.0 * cubic * before * before
    )
    return (value, slope)


def place_xy(where, core, q, r):
    dx = jnp.where(core == 0, r, q)
    dy = jnp.where(core == 0, q, r)
    return ((where[2] + dx) % N, (where[3] + dy) % N)


def dot_nt(a, b):
    return lax.dot_general(a, b, (((1,), (1,)), ((), ())), preferred_element_type=F32)


def dot_tn(a, b):
    return lax.dot_general(a, b, (((0,), (0,)), ((), ())), preferred_element_type=F32)


HBM = pl.BlockSpec(memory_space=pltpu.HBM)
ANY = pl.BlockSpec(memory_space=pl.ANY)


def relay_slot(zr, y):
    low = y < 2
    up = jnp.where(low, 12 + y, y)
    far = jnp.where(low, y, 4 + y)
    down = jnp.where(low, 4 + y, 12 + y)
    return jnp.where(zr == 0, 8 + y, jnp.where(zr == 1, up, jnp.where(zr == 2, far, down)))


def act_grad_kernel(part, where, *refs):
    own, other, weights, outs = refs[0:4], refs[4:8], refs[8:10], refs[10:12]
    lhs, w, staged, in_sems, w_sems, out_sems = refs[12:]
    columns = w.shape[2]
    loads = [
        pltpu.make_async_copy(weights[half].at[pl.ds(f * columns, columns)], w.at[f, half], w_sems.at[f, half])
        for f in range(2)
        for half in range(2)
    ]
    fills = []
    mine = pl.ds(pl.multiple_of(where[1] * K, 16), K)
    for half, stacks in enumerate((own, other)):
        for q, stack in enumerate(stacks):
            for r in range(N):
                x, y = place_xy(where, where[1] if half == 0 else 1 - where[1], q, r)
                slot = relay_slot((x + N - where[0]) % N, y) - 8 * part
                to = lhs.at[half, jnp.clip(slot, 0, 7)]
                copy = pltpu.make_async_copy(stack.at[r, mine], to, in_sems.at[half, q, r])
                fills.append(((slot >= 0) & (slot < 8), copy))
    for copy in loads[:2]:
        copy.start()
    for wanted, copy in fills:
        pl.when(wanted)(copy.start)
    for copy in loads[2:]:
        copy.start()
    for wanted, copy in fills:
        pl.when(wanted)(copy.wait)
    a, b = (lhs[half].reshape(8 * K, -1) for half in range(2))
    stores = []
    for f in range(2):
        loads[2 * f].wait()
        loads[2 * f + 1].wait()
        total = dot_nt(a, w[f, 0]) + dot_nt(b, w[f, 1])
        at = pl.ds(f * columns, columns)
        staged[:, :, at] = total.reshape(2, N * K, columns).astype(staged.dtype)
        for i in range(2):
            stores.append(pltpu.make_async_copy(staged.at[i, :, at], outs[i].at[:, at], out_sems.at[f, i]))
            stores[-1].start()
    for copy in stores:
        copy.wait()


def act_grad_parts(part, where, stacks, others, w_own, w_other):
    hidden, half = w_own.shape
    kind = (BF, F32)[part]
    return pl.pallas_call(
        functools.partial(act_grad_kernel, part),
        out_shape=[jax.ShapeDtypeStruct((N * K, hidden), kind)] * 2,
        grid_spec=pltpu.PrefetchScalarGridSpec(
            num_scalar_prefetch=1,
            grid=(),
            in_specs=[ANY] * 8 + [HBM, ANY],
            out_specs=[ANY] * 2,
            scratch_shapes=[
                pltpu.VMEM((2, 8, K, half), BF),
                pltpu.VMEM((2, 2, hidden // 2, half), BF),
                pltpu.VMEM((2, N * K, hidden), kind),
                pltpu.SemaphoreType.DMA((2, N, N)),
                pltpu.SemaphoreType.DMA((2, 2)),
                pltpu.SemaphoreType.DMA((2, 2)),
            ],
        ),
        compiler_params=pltpu.CompilerParams(vmem_limit_bytes=SMALL),
        cost_estimate=HEAVY if part else LIGHT,
        name="act_grad",
    )(where, *stacks, *others, w_own, w_other)


def input_grad_kernel(where, h0, h1, h2a, h2b, h3, w_own, w_other, *refs):
    outs, (rows_out, lhs, w, near, far, in_sems, w_sems, out_sems) = refs[:4], refs[4:]
    n = h0.shape[1]
    half = w_own.shape[0]
    rows = half
    loads = []
    for j in range(2):
        weight = (w_own, w_other)[j]
        loads.append(pltpu.make_async_copy(weight, w.at[pl.ds(j * rows, rows)], w_sems.at[j]))
    fills = []
    for zr in range(N):
        for y in range(N):
            if zr == 2:
                piece = (h2a, h2b)[y // 2].at[y % 2]
            else:
                piece = (h0, h1, None, h3)[zr].at[y]
            dx = (where[0] + zr + N - where[2]) % N
            dy = (y + N - where[3]) % N
            r = jnp.where(where[1] == 0, dx, dy)
            q = jnp.where(where[1] == 0, dy, dx)
            fills.append(pltpu.make_async_copy(piece, lhs.at[r, q], in_sems.at[zr, y]))
    for copy in loads[:1] + fills + loads[1:]:
        copy.start()
    for copy in fills:
        copy.wait()
    stores = [pltpu.make_async_copy(lhs, rows_out, out_sems.at[2, 0])]
    stores[0].start()
    for j in range(2):
        loads[j].wait()
        part = pl.ds(j * rows, rows)
        total = dot_nt(lhs[...].reshape(16 * n, -1), w[part]).reshape(N, N, n, -1)
        near[:, :, part] = total[0]
        for r in (1, 2, 3):
            far[r - 1, :, :, part] = total[r].astype(BF)
        for r in range(N):
            source = near.at[:, :, part] if r == 0 else far.at[r - 1, :, :, part]
            stores.append(pltpu.make_async_copy(source, outs[r].at[:, :, part], out_sems.at[j, r]))
            stores[-1].start()
    for copy in stores:
        copy.wait()


def input_grad_parts(where, pieces, w_own, w_other):
    half, hidden = w_own.shape
    n = pieces[0].shape[1]
    return pl.pallas_call(
        input_grad_kernel,
        out_shape=[jax.ShapeDtypeStruct((N, n, 2 * half), t) for t in (F32, BF, BF, BF)]
        + [jax.ShapeDtypeStruct((N, N, n, hidden), BF)],
        grid_spec=pltpu.PrefetchScalarGridSpec(
            num_scalar_prefetch=1,
            grid=(),
            in_specs=[HBM] * 7,
            out_specs=[HBM] * 5,
            scratch_shapes=[
                pltpu.VMEM((N, N, n, hidden), BF),
                pltpu.VMEM((2 * half, hidden), BF),
                pltpu.VMEM((N, n, 2 * half), F32),
                pltpu.VMEM((3, N, n, 2 * half), BF),
                pltpu.SemaphoreType.DMA((N, N)),
                pltpu.SemaphoreType.DMA((2,)),
                pltpu.SemaphoreType.DMA((3, N)),
            ],
        ),
        compiler_params=pltpu.CompilerParams(vmem_limit_bytes=SMALL),
        cost_estimate=LIGHT,
        name="input_grad",
    )(where, *pieces, w_own, w_other)


def weight_out_grad_kernel(where, act, g0, g1, g2, g3, out, rhs, sems):
    @pl.when(pl.program_id(0) == 0)
    def _():
        work = []
        for q, stack in enumerate((g0, g1, g2, g3)):
            for r in range(N):
                x, y = place_xy(where, where[1], q, r)
                work.append(pltpu.make_async_copy(stack.at[r], rhs.at[x, y], sems.at[q, r]))
        for copy in work:
            copy.start()
        for copy in work:
            copy.wait()

    out[...] = dot_tn(act[...], rhs[...].reshape(32 * K, -1))


def weight_out_grad_of(where, act, stacks):
    tokens, hidden = act.shape
    width = stacks[0].shape[-1]
    block = 512
    return pl.pallas_call(
        weight_out_grad_kernel,
        out_shape=jax.ShapeDtypeStruct((hidden, width), F32),
        grid_spec=pltpu.PrefetchScalarGridSpec(
            num_scalar_prefetch=1,
            grid=(hidden // block,),
            in_specs=[pl.BlockSpec((tokens, block), lambda i, s: (0, i))] + [HBM] * 4,
            out_specs=pl.BlockSpec((block, width), lambda i, s: (i, 0)),
            scratch_shapes=[pltpu.VMEM((N, N, 2 * K, width), BF), pltpu.SemaphoreType.DMA((N, N))],
        ),
        compiler_params=pltpu.CompilerParams(vmem_limit_bytes=VMEM),
        cost_estimate=HEAVY,
        name="weight_out_grad",
    )(where, act, *stacks)


def weight_in_grad_kernel(where, inputs, hid_own, hid_other, out, lhs):
    @pl.when(pl.program_id(0) == 0)
    def _():
        for s in range(2):
            core = where[1] if s == 0 else 1 - where[1]
            for r in range(N):
                for q in range(N):
                    x, y = place_xy(where, core, q, r)
                    lhs[s, r, q] = inputs[x * N + y, core]

    rows = lhs[...].reshape(2, 16 * K, -1)
    out[...] = dot_tn(rows[0], hid_own[...]) + dot_tn(rows[1], hid_other[...])


def weight_in_grad_of(where, inputs, hid_own, hid_other):
    hidden = hid_own.shape[-1]
    width = inputs.shape[1]
    block = 512
    b = pl.BlockSpec((16 * K, block), lambda i, s: (0, i))
    return pl.pallas_call(
        weight_in_grad_kernel,
        out_shape=jax.ShapeDtypeStruct((width, hidden), F32),
        grid_spec=pltpu.PrefetchScalarGridSpec(
            num_scalar_prefetch=1,
            grid=(hidden // block,),
            in_specs=[pl.BlockSpec((16, 2, K, width), lambda i, s: (0, 0, 0, 0)), b, b],
            out_specs=pl.BlockSpec((width, block), lambda i, s: (0, i)),
            scratch_shapes=[pltpu.VMEM((2, N, N, K, width), BF)],
        ),
        compiler_params=pltpu.CompilerParams(vmem_limit_bytes=VMEM),
        cost_estimate=HEAVY,
        name="weight_in_grad",
    )(where, inputs.reshape(16, 2, K, width), hid_own.reshape(-1, hidden), hid_other.reshape(-1, hidden))


def on_device(layer_input, out_grad, preactivation, weight_in, weight_out):
    row, col = lax.axis_index("row"), lax.axis_index("col")
    core = row % 2
    where = jnp.stack([row // 2, core, col // N, col % N]).astype(jnp.int32)
    width = layer_input.shape[1]
    hidden = preactivation.shape[1]

    def mine_and_other(array, axis):
        mine = lax.dynamic_index_in_dim(array, core, axis, keepdims=False)
        other = lax.dynamic_index_in_dim(array, 1 - core, axis, keepdims=False)
        return mine, swap(other)

    def in_core_order(mine, received, axis):
        return jnp.where(
            core == 0,
            jnp.concatenate([mine, received], axis),
            jnp.concatenate([received, mine], axis),
        )

    hold = lax.optimization_barrier
    act = gelu_parts(preactivation.astype(F32))[0].astype(BF)
    act_all = lax.all_gather(act, "row", axis=0, tiled=True)
    g_near = [first_ring(out_grad, -r) for r in (1, 3, 2)]
    w_out_other, w_in_other = swap(weight_out), swap(weight_in)
    g_near, w_out_other, w_in_other, preact, where = hold(
        (g_near, w_out_other, w_in_other, preactivation, where)
    )
    g_stack = jnp.stack([out_grad, g_near[0], g_near[2], g_near[1]])
    g_far = [second_ring(g_stack, -q) for q in (1, 3, 2)]
    h_set = in_core_order(*mine_and_other(preact.reshape(2, 2, K, hidden), 1), 0)
    slope = gelu_parts(h_set.astype(F32))[1]
    g_far[0], slope = hold((g_far[0], slope))
    g_stacks = [g_stack, g_far[0], g_far[2], g_far[1]]
    g_others = [swap(g) for g in g_stacks]

    half = N * K // 2
    to_up, to_down = act_grad_parts(0, where, g_stacks, g_others, weight_out, w_out_other)
    from_down, from_up = along_z(to_up, 1), along_z(to_down, -1)
    g_stacks, g_others, to_up, x_late = hold((g_stacks, g_others, to_up, layer_input))
    x_all = lax.all_gather(x_late, "col", axis=0, tiled=True)
    own, relay = act_grad_parts(1, where, g_stacks, g_others, weight_out, w_out_other)
    from_down, from_up, own, relay = hold((from_down, from_up, own, relay))
    relay_up = (relay[:half] + from_down[:half].astype(F32)).astype(BF)
    relay_down = (relay[half:] + from_up[half:].astype(F32)).astype(BF)
    sum_a, sum_b = along_z(relay_up, 1), along_z(relay_down, -1)
    rest = jnp.concatenate([from_up[:half], from_down[half:]]).astype(F32)
    act_grad = own + rest + jnp.concatenate([sum_a, sum_b]).astype(F32)
    hid = (act_grad.reshape(N, K, hidden) * slope).astype(BF)

    below, above = along_z(hid, 1), along_z(hid, -1)
    act_late, hid = hold((act_all, hid))
    weight_out_grad = weight_out_grad_of(where, act_late, g_stacks)
    below, above, weight_out_grad = hold((below, above, weight_out_grad))
    pieces = [hid, above, along_z(below[:2], 1), along_z(above[2:], -1), below]
    d0, d1, d2, d3, hid_own = input_grad_parts(where, pieces, weight_in, w_in_other)
    got = [first_ring(d, r) for r, d in ((1, d1), (3, d3), (2, d2))]
    weight_in_grad = weight_in_grad_of(where, x_all, hid_own, swap(hid_own))
    got, weight_in_grad = hold((got, weight_in_grad))

    e = d0 + got[0].astype(F32) + got[1].astype(F32) + got[2].astype(F32)
    total = e[0]
    for q in (1, 3, 2):
        total = total + second_ring(e[q].astype(BF), q).astype(F32)
    total = total.astype(BF)
    input_grad = in_core_order(total[:, :width], swap(total[:, width:]), 0)
    return (input_grad, weight_in_grad, weight_out_grad)


def solution(mesh):
    placed = (P("col", "row"), P("col", "row"), P("row", "col"), P("row", "col"), P("col", "row"))
    return jax.shard_map(
        on_device,
        mesh=mesh,
        in_specs=placed,
        out_specs=(P("col", "row"), P("row", "col"), P("col", "row")),
        check_vma=False,
    )
```

```python
import functools

import jax
import jax.numpy as jnp
from jax import lax
from jax.experimental import pallas as pl
from jax.experimental.pallas import tpu as pltpu
from jax.sharding import PartitionSpec as P

coeff = 0.7978845608
cubic = 0.044715

N = 4
K = 48
VMEM = 56 * 2**20
SMALL = 46 * 2**20
MEDIUM = 52 * 2**20
LIGHT = pl.CostEstimate(flops=1024, bytes_accessed=1024, transcendentals=0)
HEAVY = pl.CostEstimate(flops=8 * 10**9, bytes_accessed=2**24, transcendentals=0)
AXES = ("row", "col")
BF = jnp.bfloat16
F32 = jnp.float32


def permute(array, target):
    pairs = []
    for z in range(N):
        for c in range(2):
            for x in range(N):
                for y in range(N):
                    tz, tc, tx, ty = target(z, c, x, y)
                    to = (((tz % N) * 2 + tc) * N + tx % N) * N + ty % N
                    pairs.append((((z * 2 + c) * N + x) * N + y, to))
    return lax.ppermute(array, AXES, pairs)


def swap(array):
    return permute(array, lambda z, c, x, y: (z, 1 - c, x, y))


def along_z(array, by):
    return permute(array, lambda z, c, x, y: (z + by, c, x, y))


def first_ring(array, by):
    return permute(array, lambda z, c, x, y: (z, c, x, y + by) if c else (z, c, x + by, y))


def second_ring(array, by):
    return permute(array, lambda z, c, x, y: (z, c, x + by, y) if c else (z, c, x, y + by))


def gelu_parts(before):
    inner = coeff * (before + cubic * before * before * before)
    tanh_value = jnp.tanh(inner)
    value = 0.5 * before * (1.0 + tanh_value)
    slope = 0.5 * (1.0 + tanh_value) + 0.5 * before * (1.0 - tanh_value * tanh_value) * coeff * (
        1.0 + 3.0 * cubic * before * before
    )
    return (value, slope)


def place_xy(where, core, q, r):
    dx = jnp.where(core == 0, r, q)
    dy = jnp.where(core == 0, q, r)
    return ((where[2] + dx) % N, (where[3] + dy) % N)


def dot_nt(a, b):
    return lax.dot_general(a, b, (((1,), (1,)), ((), ())), preferred_element_type=F32)


def dot_tn(a, b):
    return lax.dot_general(a, b, (((0,), (0,)), ((), ())), preferred_element_type=F32)


HBM = pl.BlockSpec(memory_space=pltpu.HBM)
ANY = pl.BlockSpec(memory_space=pl.ANY)


def relay_slot(zr, y):
    low = y < 2
    up = jnp.where(low, 12 + y, y)
    far = jnp.where(low, y, 4 + y)
    down = jnp.where(low, 4 + y, 12 + y)
    return jnp.where(zr == 0, 8 + y, jnp.where(zr == 1, up, jnp.where(zr == 2, far, down)))


def act_grad_kernel(part, where, *refs):
    own, other, weights, outs = refs[0:4], refs[4:8], refs[8:10], refs[10:12]
    lhs, w, staged, in_sems, w_sems, out_sems = refs[12:]
    columns = w.shape[2]
    loads = [
        pltpu.make_async_copy(weights[half].at[pl.ds(f * columns, columns)], w.at[f, half], w_sems.at[f, half])
        for f in range(2)
        for half in range(2)
    ]
    fills = []
    mine = pl.ds(pl.multiple_of(where[1] * K, 16), K)
    for half, stacks in enumerate((own, other)):
        for q, stack in enumerate(stacks):
            for r in range(N):
                x, y = place_xy(where, where[1] if half == 0 else 1 - where[1], q, r)
                slot = relay_slot((x + N - where[0]) % N, y) - 8 * part
                to = lhs.at[half, jnp.clip(slot, 0, 7)]
                copy = pltpu.make_async_copy(stack.at[r, mine], to, in_sems.at[half, q, r])
                fills.append(((slot >= 0) & (slot < 8), copy))
    for copy in loads[:2]:
        copy.start()
    for wanted, copy in fills:
        pl.when(wanted)(copy.start)
    for copy in loads[2:]:
        copy.start()
    for wanted, copy in fills:
        pl.when(wanted)(copy.wait)
    a, b = (lhs[half].reshape(8 * K, -1) for half in range(2))
    stores = []
    for f in range(2):
        loads[2 * f].wait()
        loads[2 * f + 1].wait()
        total = dot_nt(a, w[f, 0]) + dot_nt(b, w[f, 1])
        at = pl.ds(f * columns, columns)
        staged[:, :, at] = total.reshape(2, N * K, columns).astype(staged.dtype)
        for i in range(2):
            stores.append(pltpu.make_async_copy(staged.at[i, :, at], outs[i].at[:, at], out_sems.at[f, i]))
            stores[-1].start()
    for copy in stores:
        copy.wait()


def act_grad_parts(part, where, stacks, others, w_own, w_other):
    hidden, half = w_own.shape
    kind = (BF, F32)[part]
    return pl.pallas_call(
        functools.partial(act_grad_kernel, part),
        out_shape=[jax.ShapeDtypeStruct((N * K, hidden), kind)] * 2,
        grid_spec=pltpu.PrefetchScalarGridSpec(
            num_scalar_prefetch=1,
            grid=(),
            in_specs=[ANY] * 8 + [HBM, ANY],
            out_specs=[ANY] * 2,
            scratch_shapes=[
                pltpu.VMEM((2, 8, K, half), BF),
                pltpu.VMEM((2, 2, hidden // 2, half), BF),
                pltpu.VMEM((2, N * K, hidden), kind),
                pltpu.SemaphoreType.DMA((2, N, N)),
                pltpu.SemaphoreType.DMA((2, 2)),
                pltpu.SemaphoreType.DMA((2, 2)),
            ],
        ),
        compiler_params=pltpu.CompilerParams(vmem_limit_bytes=SMALL),
        cost_estimate=HEAVY if part else LIGHT,
        name="act_grad",
    )(where, *stacks, *others, w_own, w_other)


def input_grad_kernel(where, h0, h1, h2a, h2b, h3, w_own, w_other, *refs):
    outs, (rows_out, lhs, w, near, far, in_sems, w_sems, out_sems) = refs[:4], refs[4:]
    n = h0.shape[1]
    half = w_own.shape[0]
    rows = half
    loads = []
    for j in range(2):
        weight = (w_own, w_other)[j]
        loads.append(pltpu.make_async_copy(weight, w.at[pl.ds(j * rows, rows)], w_sems.at[j]))
    fills = []
    for zr in range(N):
        for y in range(N):
            if zr == 2:
                piece = (h2a, h2b)[y // 2].at[y % 2]
            else:
                piece = (h0, h1, None, h3)[zr].at[y]
            dx = (where[0] + zr + N - where[2]) % N
            dy = (y + N - where[3]) % N
            r = jnp.where(where[1] == 0, dx, dy)
            q = jnp.where(where[1] == 0, dy, dx)
            fills.append(pltpu.make_async_copy(piece, lhs.at[r, q], in_sems.at[zr, y]))
    for copy in loads[:1] + fills + loads[1:]:
        copy.start()
    for copy in fills:
        copy.wait()
    stores = [pltpu.make_async_copy(lhs, rows_out, out_sems.at[2, 0])]
    stores[0].start()
    for j in range(2):
        loads[j].wait()
        part = pl.ds(j * rows, rows)
        total = dot_nt(lhs[...].reshape(16 * n, -1), w[part]).reshape(N, N, n, -1)
        near[:, :, part] = total[0]
        for r in (1, 2, 3):
            far[r - 1, :, :, part] = total[r].astype(BF)
        for r in range(N):
            source = near.at[:, :, part] if r == 0 else far.at[r - 1, :, :, part]
            stores.append(pltpu.make_async_copy(source, outs[r].at[:, :, part], out_sems.at[j, r]))
            stores[-1].start()
    for copy in stores:
        copy.wait()


def input_grad_parts(where, pieces, w_own, w_other):
    half, hidden = w_own.shape
    n = pieces[0].shape[1]
    return pl.pallas_call(
        input_grad_kernel,
        out_shape=[jax.ShapeDtypeStruct((N, n, 2 * half), t) for t in (F32, BF, BF, BF)]
        + [jax.ShapeDtypeStruct((N, N, n, hidden), BF)],
        grid_spec=pltpu.PrefetchScalarGridSpec(
            num_scalar_prefetch=1,
            grid=(),
            in_specs=[HBM] * 7,
            out_specs=[HBM] * 5,
            scratch_shapes=[
                pltpu.VMEM((N, N, n, hidden), BF),
                pltpu.VMEM((2 * half, hidden), BF),
                pltpu.VMEM((N, n, 2 * half), F32),
                pltpu.VMEM((3, N, n, 2 * half), BF),
                pltpu.SemaphoreType.DMA((N, N)),
                pltpu.SemaphoreType.DMA((2,)),
                pltpu.SemaphoreType.DMA((3, N)),
            ],
        ),
        compiler_params=pltpu.CompilerParams(vmem_limit_bytes=MEDIUM),
        cost_estimate=LIGHT,
        name="input_grad",
    )(where, *pieces, w_own, w_other)


def weight_out_grad_kernel(where, act, g0, g1, g2, g3, out, rhs, sems):
    @pl.when(pl.program_id(0) == 0)
    def _():
        work = []
        for q, stack in enumerate((g0, g1, g2, g3)):
            for r in range(N):
                x, y = place_xy(where, where[1], q, r)
                work.append(pltpu.make_async_copy(stack.at[r], rhs.at[x, y], sems.at[q, r]))
        for copy in work:
            copy.start()
        for copy in work:
            copy.wait()

    out[...] = dot_tn(act[...], rhs[...].reshape(32 * K, -1))


def weight_out_grad_of(where, act, stacks):
    tokens, hidden = act.shape
    width = stacks[0].shape[-1]
    block = 512
    return pl.pallas_call(
        weight_out_grad_kernel,
        out_shape=jax.ShapeDtypeStruct((hidden, width), F32),
        grid_spec=pltpu.PrefetchScalarGridSpec(
            num_scalar_prefetch=1,
            grid=(hidden // block,),
            in_specs=[pl.BlockSpec((tokens, block), lambda i, s: (0, i))] + [HBM] * 4,
            out_specs=pl.BlockSpec((block, width), lambda i, s: (i, 0)),
            scratch_shapes=[pltpu.VMEM((N, N, 2 * K, width), BF), pltpu.SemaphoreType.DMA((N, N))],
        ),
        compiler_params=pltpu.CompilerParams(vmem_limit_bytes=VMEM),
        cost_estimate=HEAVY,
        name="weight_out_grad",
    )(where, act, *stacks)


def weight_in_grad_kernel(where, inputs, hid_own, hid_other, out, lhs):
    @pl.when(pl.program_id(0) == 0)
    def _():
        for s in range(2):
            core = where[1] if s == 0 else 1 - where[1]
            for r in range(N):
                for q in range(N):
                    x, y = place_xy(where, core, q, r)
                    lhs[s, r, q] = inputs[x * N + y, core]

    rows = lhs[...].reshape(2, 16 * K, -1)
    out[...] = dot_tn(rows[0], hid_own[...]) + dot_tn(rows[1], hid_other[...])


def weight_in_grad_of(where, inputs, hid_own, hid_other):
    hidden = hid_own.shape[-1]
    width = inputs.shape[1]
    block = 512
    b = pl.BlockSpec((16 * K, block), lambda i, s: (0, i))
    return pl.pallas_call(
        weight_in_grad_kernel,
        out_shape=jax.ShapeDtypeStruct((width, hidden), F32),
        grid_spec=pltpu.PrefetchScalarGridSpec(
            num_scalar_prefetch=1,
            grid=(hidden // block,),
            in_specs=[pl.BlockSpec((16, 2, K, width), lambda i, s: (0, 0, 0, 0)), b, b],
            out_specs=pl.BlockSpec((width, block), lambda i, s: (0, i)),
            scratch_shapes=[pltpu.VMEM((2, N, N, K, width), BF)],
        ),
        compiler_params=pltpu.CompilerParams(vmem_limit_bytes=VMEM),
        cost_estimate=HEAVY,
        name="weight_in_grad",
    )(where, inputs.reshape(16, 2, K, width), hid_own.reshape(-1, hidden), hid_other.reshape(-1, hidden))


def on_device(layer_input, out_grad, preactivation, weight_in, weight_out):
    row, col = lax.axis_index("row"), lax.axis_index("col")
    core = row % 2
    where = jnp.stack([row // 2, core, col // N, col % N]).astype(jnp.int32)
    width = layer_input.shape[1]
    hidden = preactivation.shape[1]

    def mine_and_other(array, axis):
        mine = lax.dynamic_index_in_dim(array, core, axis, keepdims=False)
        other = lax.dynamic_index_in_dim(array, 1 - core, axis, keepdims=False)
        return mine, swap(other)

    def in_core_order(mine, received, axis):
        return jnp.where(
            core == 0,
            jnp.concatenate([mine, received], axis),
            jnp.concatenate([received, mine], axis),
        )

    hold = lax.optimization_barrier
    act = gelu_parts(preactivation.astype(F32))[0].astype(BF)
    act_all = lax.all_gather(act, "row", axis=0, tiled=True)
    g_near = [first_ring(out_grad, -r) for r in (1, 3, 2)]
    w_out_other, w_in_other = swap(weight_out), swap(weight_in)
    g_near, w_out_other, w_in_other, preact, where = hold(
        (g_near, w_out_other, w_in_other, preactivation, where)
    )
    g_stack = jnp.stack([out_grad, g_near[0], g_near[2], g_near[1]])
    g_far = [second_ring(g_stack, -q) for q in (1, 3, 2)]
    h_set = in_core_order(*mine_and_other(preact.reshape(2, 2, K, hidden), 1), 0)
    slope = gelu_parts(h_set.astype(F32))[1]
    g_far[0], slope = hold((g_far[0], slope))
    g_stacks = [g_stack, g_far[0], g_far[2], g_far[1]]
    g_others = [swap(g) for g in g_stacks]

    half = N * K // 2
    to_up, to_down = act_grad_parts(0, where, g_stacks, g_others, weight_out, w_out_other)
    from_down, from_up = along_z(to_up, 1), along_z(to_down, -1)
    g_stacks, g_others, to_up, x_late = hold((g_stacks, g_others, to_up, layer_input))
    x_all = lax.all_gather(x_late, "col", axis=0, tiled=True)
    own, relay = act_grad_parts(1, where, g_stacks, g_others, weight_out, w_out_other)
    from_down, from_up, own, relay = hold((from_down, from_up, own, relay))
    relay_up = (relay[:half] + from_down[:half].astype(F32)).astype(BF)
    relay_down = (relay[half:] + from_up[half:].astype(F32)).astype(BF)
    sum_a, sum_b = along_z(relay_up, 1), along_z(relay_down, -1)
    rest = jnp.concatenate([from_up[:half], from_down[half:]]).astype(F32)
    act_grad = own + rest + jnp.concatenate([sum_a, sum_b]).astype(F32)
    hid = (act_grad.reshape(N, K, hidden) * slope).astype(BF)

    below, above = along_z(hid, 1), along_z(hid, -1)
    act_late, hid = hold((act_all, hid))
    weight_out_grad = weight_out_grad_of(where, act_late, g_stacks)
    below, above, weight_out_grad = hold((below, above, weight_out_grad))
    pieces = [hid, above, along_z(below[:2], 1), along_z(above[2:], -1), below]
    d0, d1, d2, d3, hid_own = input_grad_parts(where, pieces, weight_in, w_in_other)
    got = [first_ring(d, r) for r, d in ((1, d1), (3, d3), (2, d2))]
    weight_in_grad = weight_in_grad_of(where, x_all, hid_own, swap(hid_own))
    got, weight_in_grad = hold((got, weight_in_grad))

    e = d0 + got[0].astype(F32) + got[1].astype(F32) + got[2].astype(F32)
    total = e[0]
    for q in (1, 3, 2):
        total = total + second_ring(e[q].astype(BF), q).astype(F32)
    total = total.astype(BF)
    input_grad = in_core_order(total[:, :width], swap(total[:, width:]), 0)
    return (input_grad, weight_in_grad, weight_out_grad)


def solution(mesh):
    placed = (P("col", "row"), P("col", "row"), P("row", "col"), P("row", "col"), P("col", "row"))
    return jax.shard_map(
        on_device,
        mesh=mesh,
        in_specs=placed,
        out_specs=(P("col", "row"), P("row", "col"), P("col", "row")),
        check_vma=False,
    )
```

```python
import functools

import jax
import jax.numpy as jnp
from jax import lax
from jax.experimental import pallas as pl
from jax.experimental.pallas import tpu as pltpu
from jax.sharding import PartitionSpec as P

coeff = 0.7978845608
cubic = 0.044715

N = 4
K = 48
VMEM = 56 * 2**20
SMALL = 46 * 2**20
MEDIUM = 52 * 2**20
LIGHT = pl.CostEstimate(flops=1024, bytes_accessed=1024, transcendentals=0)
HEAVY = pl.CostEstimate(flops=8 * 10**9, bytes_accessed=2**24, transcendentals=0)
AXES = ("row", "col")
BF = jnp.bfloat16
F32 = jnp.float32


def permute(array, target):
    pairs = []
    for z in range(N):
        for c in range(2):
            for x in range(N):
                for y in range(N):
                    tz, tc, tx, ty = target(z, c, x, y)
                    to = (((tz % N) * 2 + tc) * N + tx % N) * N + ty % N
                    pairs.append((((z * 2 + c) * N + x) * N + y, to))
    return lax.ppermute(array, AXES, pairs)


def swap(array):
    return permute(array, lambda z, c, x, y: (z, 1 - c, x, y))


def along_z(array, by):
    return permute(array, lambda z, c, x, y: (z + by, c, x, y))


def first_ring(array, by):
    return permute(array, lambda z, c, x, y: (z, c, x, y + by) if c else (z, c, x + by, y))


def second_ring(array, by):
    return permute(array, lambda z, c, x, y: (z, c, x + by, y) if c else (z, c, x, y + by))


def gelu_parts(before):
    inner = coeff * (before + cubic * before * before * before)
    tanh_value = jnp.tanh(inner)
    value = 0.5 * before * (1.0 + tanh_value)
    slope = 0.5 * (1.0 + tanh_value) + 0.5 * before * (1.0 - tanh_value * tanh_value) * coeff * (
        1.0 + 3.0 * cubic * before * before
    )
    return (value, slope)


def place_xy(where, core, q, r):
    dx = jnp.where(core == 0, r, q)
    dy = jnp.where(core == 0, q, r)
    return ((where[2] + dx) % N, (where[3] + dy) % N)


def dot_nt(a, b):
    return lax.dot_general(a, b, (((1,), (1,)), ((), ())), preferred_element_type=F32)


def dot_tn(a, b):
    return lax.dot_general(a, b, (((0,), (0,)), ((), ())), preferred_element_type=F32)


HBM = pl.BlockSpec(memory_space=pltpu.HBM)
ANY = pl.BlockSpec(memory_space=pl.ANY)


def relay_slot(zr, y):
    low = y < 2
    up = jnp.where(low, 12 + y, y)
    far = jnp.where(low, y, 4 + y)
    down = jnp.where(low, 4 + y, 12 + y)
    return jnp.where(zr == 0, 8 + y, jnp.where(zr == 1, up, jnp.where(zr == 2, far, down)))


def act_grad_kernel(part, where, *refs):
    own, other, weights, outs = refs[0:4], refs[4:8], refs[8:10], refs[10:12]
    lhs, w, staged, in_sems, w_sems, out_sems = refs[12:]
    columns = w.shape[2]
    loads = [
        pltpu.make_async_copy(weights[half].at[pl.ds(f * columns, columns)], w.at[f, half], w_sems.at[f, half])
        for f in range(2)
        for half in range(2)
    ]
    fills = []
    mine = pl.ds(pl.multiple_of(where[1] * K, 16), K)
    for half, stacks in enumerate((own, other)):
        for q, stack in enumerate(stacks):
            for r in range(N):
                x, y = place_xy(where, where[1] if half == 0 else 1 - where[1], q, r)
                slot = relay_slot((x + N - where[0]) % N, y) - 8 * part
                to = lhs.at[half, jnp.clip(slot, 0, 7)]
                copy = pltpu.make_async_copy(stack.at[r, mine], to, in_sems.at[half, q, r])
                fills.append(((slot >= 0) & (slot < 8), copy))
    for copy in loads[:2]:
        copy.start()
    for wanted, copy in fills:
        pl.when(wanted)(copy.start)
    for copy in loads[2:]:
        copy.start()
    for wanted, copy in fills:
        pl.when(wanted)(copy.wait)
    a, b = (lhs[half].reshape(8 * K, -1) for half in range(2))
    stores = []
    for f in range(2):
        loads[2 * f].wait()
        loads[2 * f + 1].wait()
        total = dot_nt(a, w[f, 0]) + dot_nt(b, w[f, 1])
        at = pl.ds(f * columns, columns)
        staged[:, :, at] = total.reshape(2, N * K, columns).astype(staged.dtype)
        for i in range(2):
            stores.append(pltpu.make_async_copy(staged.at[i, :, at], outs[i].at[:, at], out_sems.at[f, i]))
            stores[-1].start()
    for copy in stores:
        copy.wait()


def act_grad_parts(part, where, stacks, others, w_own, w_other):
    hidden, half = w_own.shape
    kind = (BF, F32)[part]
    return pl.pallas_call(
        functools.partial(act_grad_kernel, part),
        out_shape=[jax.ShapeDtypeStruct((N * K, hidden), kind)] * 2,
        grid_spec=pltpu.PrefetchScalarGridSpec(
            num_scalar_prefetch=1,
            grid=(),
            in_specs=[ANY] * 8 + [HBM, ANY],
            out_specs=[ANY] * 2,
            scratch_shapes=[
                pltpu.VMEM((2, 8, K, half), BF),
                pltpu.VMEM((2, 2, hidden // 2, half), BF),
                pltpu.VMEM((2, N * K, hidden), kind),
                pltpu.SemaphoreType.DMA((2, N, N)),
                pltpu.SemaphoreType.DMA((2, 2)),
                pltpu.SemaphoreType.DMA((2, 2)),
            ],
        ),
        compiler_params=pltpu.CompilerParams(vmem_limit_bytes=SMALL),
        cost_estimate=HEAVY if part else LIGHT,
        name="act_grad",
    )(where, *stacks, *others, w_own, w_other)


def input_grad_kernel(where, h0, h1, h2a, h2b, h3, w_own, w_other, *refs):
    outs, (rows_out, lhs, w, near, far, in_sems, w_sems, out_sems) = refs[:4], refs[4:]
    n = h0.shape[1]
    half = w_own.shape[0]
    rows = half
    loads = []
    for j in range(2):
        weight = (w_own, w_other)[j]
        loads.append(pltpu.make_async_copy(weight, w.at[pl.ds(j * rows, rows)], w_sems.at[j]))
    fills = []
    for zr in range(N):
        for y in range(N):
            if zr == 2:
                piece = (h2a, h2b)[y // 2].at[y % 2]
            else:
                piece = (h0, h1, None, h3)[zr].at[y]
            dx = (where[0] + zr + N - where[2]) % N
            dy = (y + N - where[3]) % N
            r = jnp.where(where[1] == 0, dx, dy)
            q = jnp.where(where[1] == 0, dy, dx)
            fills.append(pltpu.make_async_copy(piece, lhs.at[r, q], in_sems.at[zr, y]))
    for copy in loads[:1] + fills + loads[1:]:
        copy.start()
    for copy in fills:
        copy.wait()
    rows_copy = pltpu.make_async_copy(lhs, rows_out, out_sems.at[2, 0])
    stores = [rows_copy]
    for j in range(2):
        loads[j].wait()
        part = pl.ds(j * rows, rows)
        if j == 1:
            rows_copy.start()
        total = dot_nt(lhs[...].reshape(16 * n, -1), w[part]).reshape(N, N, n, -1)
        near[:, :, part] = total[0]
        for r in (1, 2, 3):
            far[r - 1, :, :, part] = total[r].astype(BF)
        for r in range(N):
            source = near.at[:, :, part] if r == 0 else far.at[r - 1, :, :, part]
            stores.append(pltpu.make_async_copy(source, outs[r].at[:, :, part], out_sems.at[j, r]))
            stores[-1].start()
    for copy in stores:
        copy.wait()


def input_grad_parts(where, pieces, w_own, w_other):
    half, hidden = w_own.shape
    n = pieces[0].shape[1]
    return pl.pallas_call(
        input_grad_kernel,
        out_shape=[jax.ShapeDtypeStruct((N, n, 2 * half), t) for t in (F32, BF, BF, BF)]
        + [jax.ShapeDtypeStruct((N, N, n, hidden), BF)],
        grid_spec=pltpu.PrefetchScalarGridSpec(
            num_scalar_prefetch=1,
            grid=(),
            in_specs=[HBM] * 7,
            out_specs=[HBM] * 5,
            scratch_shapes=[
                pltpu.VMEM((N, N, n, hidden), BF),
                pltpu.VMEM((2 * half, hidden), BF),
                pltpu.VMEM((N, n, 2 * half), F32),
                pltpu.VMEM((3, N, n, 2 * half), BF),
                pltpu.SemaphoreType.DMA((N, N)),
                pltpu.SemaphoreType.DMA((2,)),
                pltpu.SemaphoreType.DMA((3, N)),
            ],
        ),
        compiler_params=pltpu.CompilerParams(vmem_limit_bytes=MEDIUM),
        cost_estimate=LIGHT,
        name="input_grad",
    )(where, *pieces, w_own, w_other)


def weight_out_grad_kernel(where, act, g0, g1, g2, g3, out, rhs, sems):
    @pl.when(pl.program_id(0) == 0)
    def _():
        work = []
        for q, stack in enumerate((g0, g1, g2, g3)):
            for r in range(N):
                x, y = place_xy(where, where[1], q, r)
                work.append(pltpu.make_async_copy(stack.at[r], rhs.at[x, y], sems.at[q, r]))
        for copy in work:
            copy.start()
        for copy in work:
            copy.wait()

    out[...] = dot_tn(act[...], rhs[...].reshape(32 * K, -1))


def weight_out_grad_of(where, act, stacks):
    tokens, hidden = act.shape
    width = stacks[0].shape[-1]
    block = 512
    return pl.pallas_call(
        weight_out_grad_kernel,
        out_shape=jax.ShapeDtypeStruct((hidden, width), F32),
        grid_spec=pltpu.PrefetchScalarGridSpec(
            num_scalar_prefetch=1,
            grid=(hidden // block,),
            in_specs=[pl.BlockSpec((tokens, block), lambda i, s: (0, i))] + [HBM] * 4,
            out_specs=pl.BlockSpec((block, width), lambda i, s: (i, 0)),
            scratch_shapes=[pltpu.VMEM((N, N, 2 * K, width), BF), pltpu.SemaphoreType.DMA((N, N))],
        ),
        compiler_params=pltpu.CompilerParams(vmem_limit_bytes=VMEM),
        cost_estimate=HEAVY,
        name="weight_out_grad",
    )(where, act, *stacks)


def weight_in_grad_kernel(where, inputs, hid_own, hid_other, out, lhs):
    @pl.when(pl.program_id(0) == 0)
    def _():
        for s in range(2):
            core = where[1] if s == 0 else 1 - where[1]
            for r in range(N):
                for q in range(N):
                    x, y = place_xy(where, core, q, r)
                    lhs[s, r, q] = inputs[x * N + y, core]

    rows = lhs[...].reshape(2, 16 * K, -1)
    out[...] = dot_tn(rows[0], hid_own[...]) + dot_tn(rows[1], hid_other[...])


def weight_in_grad_of(where, inputs, hid_own, hid_other):
    hidden = hid_own.shape[-1]
    width = inputs.shape[1]
    block = 512
    b = pl.BlockSpec((16 * K, block), lambda i, s: (0, i))
    return pl.pallas_call(
        weight_in_grad_kernel,
        out_shape=jax.ShapeDtypeStruct((width, hidden), F32),
        grid_spec=pltpu.PrefetchScalarGridSpec(
            num_scalar_prefetch=1,
            grid=(hidden // block,),
            in_specs=[pl.BlockSpec((16, 2, K, width), lambda i, s: (0, 0, 0, 0)), b, b],
            out_specs=pl.BlockSpec((width, block), lambda i, s: (0, i)),
            scratch_shapes=[pltpu.VMEM((2, N, N, K, width), BF)],
        ),
        compiler_params=pltpu.CompilerParams(vmem_limit_bytes=VMEM),
        cost_estimate=HEAVY,
        name="weight_in_grad",
    )(where, inputs.reshape(16, 2, K, width), hid_own.reshape(-1, hidden), hid_other.reshape(-1, hidden))


def on_device(layer_input, out_grad, preactivation, weight_in, weight_out):
    row, col = lax.axis_index("row"), lax.axis_index("col")
    core = row % 2
    where = jnp.stack([row // 2, core, col // N, col % N]).astype(jnp.int32)
    width = layer_input.shape[1]
    hidden = preactivation.shape[1]

    def mine_and_other(array, axis):
        mine = lax.dynamic_index_in_dim(array, core, axis, keepdims=False)
        other = lax.dynamic_index_in_dim(array, 1 - core, axis, keepdims=False)
        return mine, swap(other)

    def in_core_order(mine, received, axis):
        return jnp.where(
            core == 0,
            jnp.concatenate([mine, received], axis),
            jnp.concatenate([received, mine], axis),
        )

    hold = lax.optimization_barrier
    act = gelu_parts(preactivation.astype(F32))[0].astype(BF)
    act_all = lax.all_gather(act, "row", axis=0, tiled=True)
    g_near = [first_ring(out_grad, -r) for r in (1, 3, 2)]
    w_out_other, w_in_other = swap(weight_out), swap(weight_in)
    g_near, w_out_other, w_in_other, preact, where = hold(
        (g_near, w_out_other, w_in_other, preactivation, where)
    )
    g_stack = jnp.stack([out_grad, g_near[0], g_near[2], g_near[1]])
    g_far = [second_ring(g_stack, -q) for q in (1, 3, 2)]
    h_set = in_core_order(*mine_and_other(preact.reshape(2, 2, K, hidden), 1), 0)
    slope = gelu_parts(h_set.astype(F32))[1]
    g_far[0], slope = hold((g_far[0], slope))
    g_stacks = [g_stack, g_far[0], g_far[2], g_far[1]]
    g_others = [swap(g) for g in g_stacks]

    half = N * K // 2
    to_up, to_down = act_grad_parts(0, where, g_stacks, g_others, weight_out, w_out_other)
    from_down, from_up = along_z(to_up, 1), along_z(to_down, -1)
    g_stacks, g_others, to_up, x_late = hold((g_stacks, g_others, to_up, layer_input))
    x_all = lax.all_gather(x_late, "col", axis=0, tiled=True)
    own, relay = act_grad_parts(1, where, g_stacks, g_others, weight_out, w_out_other)
    from_down, from_up, own, relay = hold((from_down, from_up, own, relay))
    relay_up = (relay[:half] + from_down[:half].astype(F32)).astype(BF)
    relay_down = (relay[half:] + from_up[half:].astype(F32)).astype(BF)
    sum_a, sum_b = along_z(relay_up, 1), along_z(relay_down, -1)
    rest = jnp.concatenate([from_up[:half], from_down[half:]]).astype(F32)
    act_grad = own + rest + jnp.concatenate([sum_a, sum_b]).astype(F32)
    hid = (act_grad.reshape(N, K, hidden) * slope).astype(BF)

    below, above = along_z(hid, 1), along_z(hid, -1)
    act_late, hid = hold((act_all, hid))
    weight_out_grad = weight_out_grad_of(where, act_late, g_stacks)
    below, above, weight_out_grad = hold((below, above, weight_out_grad))
    pieces = [hid, above, along_z(below[:2], 1), along_z(above[2:], -1), below]
    d0, d1, d2, d3, hid_own = input_grad_parts(where, pieces, weight_in, w_in_other)
    got = [first_ring(d, r) for r, d in ((1, d1), (3, d3), (2, d2))]
    weight_in_grad = weight_in_grad_of(where, x_all, hid_own, swap(hid_own))
    got, weight_in_grad = hold((got, weight_in_grad))

    e = d0 + got[0].astype(F32) + got[1].astype(F32) + got[2].astype(F32)
    total = e[0]
    for q in (1, 3, 2):
        total = total + second_ring(e[q].astype(BF), q).astype(F32)
    total = total.astype(BF)
    input_grad = in_core_order(total[:, :width], swap(total[:, width:]), 0)
    return (input_grad, weight_in_grad, weight_out_grad)


def solution(mesh):
    placed = (P("col", "row"), P("col", "row"), P("row", "col"), P("row", "col"), P("col", "row"))
    return jax.shard_map(
        on_device,
        mesh=mesh,
        in_specs=placed,
        out_specs=(P("col", "row"), P("row", "col"), P("col", "row")),
        check_vma=False,
    )
```
